32 devices in a mesh: groups: 2 (over y), paths: 4 (over z), mp: 2 (over x), pipe: 2 (over core).
Axes of the slice: x: 2, y: 2, z: 4, core: 2. Of those that a mesh axis runs over, the one named last changes fastest.
Arguments:
- inputs: bfloat16 [4096, 1024], P(('groups', 'paths', 'pipe'), 'mp'), parts along dimension 0, may hold values from -6 to 6
- cotangent: bfloat16 [4096, 1024], P(('groups', 'paths', 'pipe'), 'mp'), parts along dimension 0, may hold values from -6 to 6
- path_table: int32 [8, 2], P('groups'), parts along dimension 0, may hold values from 0 to 1
- slot_module: int32 [4], replicated, may hold values from 0 to 3, each once
- weights: bfloat16 [4, 2, 1024, 4096], P('paths', None, 'pipe', 'mp'), may hold values from -0.09375 to 0.09375
- momentum: bfloat16 [4, 2, 1024, 4096], P('paths', None, 'pipe', 'mp'), may hold values from -6 to 6
- row_factor: float32 [8, 2, 2, 1024], P(('groups', 'paths'), None, None, 'pipe'), parts along dimension 0, may hold values from 1 to 16
- col_factor: float32 [8, 2, 2, 4096], P(('groups', 'paths'), None, None, 'mp'), parts along dimension 0, may hold values from 1 to 16
Outputs:
- new_momentum: bfloat16 [8, 2, 1024, 4096], P(('groups', 'paths'), None, 'pipe', 'mp'), parts along dimension 0
- nesterov_step: bfloat16 [8, 2, 1024, 4096], P(('groups', 'paths'), None, 'pipe', 'mp'), parts along dimension 0
The draws below stay inside these ranges and needn't reach their ends.
There are 2 independent parts, one for each index of `groups`. The reference program is written for one: setup_inputs(seed, part) draws one part's arguments, and reference() takes and returns one part's arrays. A program takes and returns all parts, laid end to end along the dimension named above; an argument that names none is the same for every part. Nothing has to cross between parts.
Inputs may be any that keep to these rules, and one draw needn't show every extreme that they name: `path_table`: each entry names a module by its index within its level. `slot_module`: a permutation: each module is held in exactly one slot.
All inputs are finite; a program needn't handle non-finite values.
Results may differ from the reference program's by a relative error of at most 0.014.
Values may be sent and summed in bfloat16 or wider, within the bound.
A program may use at most 128 MiB of HBM per device.

```python
import math
import jax
import jax.numpy as jnp
import numpy as np
from jax import lax

D = 1024
FF = 4096
LEVELS = 2
TOK_DEV = 256
PATHS = 4
MODULES = 4
PER_LEVEL = 2
TOK_PATH = 512
TOKENS = 2048
N_MP = 2
N_PIPE = 2


def set_ends(result, stream_key, least, high):
    extent = result.shape
    place = [jax.random.randint(jax.random.fold_in(stream_key, axis), (), 0, extent[axis]) for axis in range(len(extent))]
    result = result.at[tuple(place)].set(least)
    longest = extent.index(max(extent))
    place[longest] = (place[longest] + 1) % extent[longest]
    return result.at[tuple(place)].set(high)


def level_of(rng, shape, split, low, top_value):
    level = 1.0
    for position, parts in split:
        heights = jax.random.uniform(jax.random.fold_in(jax.random.fold_in(rng, 6), position), (parts,), jnp.float32, low / len(split), top_value / len(split))
        level = level * jnp.repeat(jnp.exp(heights), shape[position] // parts).reshape((-1,) + (1,) * (len(shape) - 1 - position))
    return level


def rank_table(number_of, skew):
    weights = [(1 << 20) // math.isqrt(grade ** skew) + 1 for grade in range(1, number_of + 1)]
    scale = 1 + sum(weights) // (1 << 30)
    return np.cumsum(np.array([max(1, weight // scale) for weight in weights]))


def ranked_ids(stream_key, dims, amount, lean):
    table = rank_table(amount, lean)
    lot = jax.random.randint(jax.random.fold_in(stream_key, 1), dims, 0, int(table[amount - 1]))
    rank = jnp.searchsorted(jnp.asarray(table, jnp.int32), lot, side="right")
    return jax.random.permutation(jax.random.fold_in(stream_key, 2), amount)[rank].astype(jnp.int32)


def bell_draw(own_key, shape, deviation, most, cuts=(), kind=jnp.bfloat16):
    values = deviation * jax.random.normal(own_key, shape, jnp.float32)
    if cuts:
        values = values * level_of(own_key, shape, cuts, -0.22, 0.18)
    return jnp.clip(values, -most, most).astype(kind)


def setup_inputs(seed: int = 0, part: int = 0) -> dict:
    splits = jax.random.split(jax.random.key(seed), 9)
    part_keys = jax.random.split(jax.random.fold_in(splits[8], part), 9)
    return {
        "inputs": bell_draw(part_keys[0], (TOKENS, D), 1.0, 6.0, ((0, 8), (1, 2))),
        "cotangent": bell_draw(part_keys[1], (TOKENS, D), 1.0, 6.0, ((0, 8), (1, 2))),
        "path_table": set_ends(ranked_ids(part_keys[2], (PATHS, LEVELS), PER_LEVEL, 1), jax.random.fold_in(part_keys[2], 3), 0, PER_LEVEL - 1).astype(jnp.int32),
        "slot_module": jax.random.permutation(splits[3], MODULES).astype(jnp.int32),
        "weights": bell_draw(splits[4], (MODULES, 2, D, FF), FF ** -0.5, 0.09375, ((0, 4), (2, 2), (3, 2))),
        "momentum": bell_draw(splits[5], (MODULES, 2, D, FF), 1.0, 6.0, ((0, 4), (2, 2), (3, 2))),
        "row_factor": jnp.clip(jnp.exp(math.log(16.0) - 2.7725887 * jax.random.uniform(part_keys[6], (PATHS, LEVELS, 2, D), jnp.float32) ** level_of(part_keys[6], (PATHS, LEVELS, 2, D), ((0, 4), (3, 2)), -0.2, 0.2)), 1.0, 16.0),
        "col_factor": jnp.clip(jnp.exp(math.log(16.0) - 2.7725887 * jax.random.uniform(part_keys[7], (PATHS, LEVELS, 2, FF), jnp.float32) ** level_of(part_keys[7], (PATHS, LEVELS, 2, FF), ((0, 4), (3, 2)), -0.2, 0.2)), 1.0, 16.0),
    }


norm_eps = 1e-06
beta_two = 0.95
adam_eps = 1e-08
momentum_mu = 0.9

def gelu_tanh(values):
    return jax.nn.gelu(values, approximate=True)

def hidden_blocks(left, matrix):
    rows = left.shape[0]
    block = FF // N_MP
    left_f = left.astype(jnp.float32).reshape(rows, N_MP, block)
    right_f = matrix.astype(jnp.float32).reshape(matrix.shape[0], N_MP, block)
    partials = jnp.einsum('tkf,dkf->ktd', left_f, right_f)
    return lax.optimization_barrier(jnp.sum(partials.astype(jnp.bfloat16).astype(jnp.float32), axis=0))

def token_blocks(left, right):
    left_f = left.astype(jnp.float32).reshape(N_PIPE, TOK_DEV, left.shape[1])
    right_f = right.astype(jnp.float32).reshape(N_PIPE, TOK_DEV, right.shape[1])
    partials = jnp.einsum('ptd,ptf->pdf', left_f, right_f)
    return lax.optimization_barrier(jnp.sum(partials.astype(jnp.bfloat16).astype(jnp.float32), axis=0))

def path_deltas(path_inputs, path_cot, module_w, path_rows, path_cols):
    stream = path_inputs.astype(jnp.float32)
    saved = []
    for level in range(LEVELS):
        up_w = module_w[level, 0]
        down_w = module_w[level, 1]
        inv_rms = lax.rsqrt(lax.optimization_barrier(jnp.mean(stream * stream, axis=1, keepdims=True)) + norm_eps)
        normed = stream * inv_rms
        normed_b = normed.astype(jnp.bfloat16)
        pre_act = jnp.dot(normed_b, up_w, preferred_element_type=jnp.float32)
        activated = gelu_tanh(pre_act).astype(jnp.bfloat16)
        saved.append((inv_rms, normed, normed_b, pre_act, activated))
        stream = stream + hidden_blocks(activated, down_w)
    stream_grad = path_cot.astype(jnp.float32)
    grads = [None] * LEVELS
    for level in reversed(range(LEVELS)):
        inv_rms, normed, normed_b, pre_act, activated = saved[level]
        up_w = module_w[level, 0]
        down_w = module_w[level, 1]
        out_grad = stream_grad.astype(jnp.bfloat16)
        act_grad = jnp.dot(out_grad, down_w, preferred_element_type=jnp.float32)
        pre_grad = jax.vjp(gelu_tanh, pre_act)[1](act_grad)[0].astype(jnp.bfloat16)
        grads[level] = jnp.stack([token_blocks(normed_b, pre_grad), token_blocks(out_grad, activated)])
        if level > 0:
            norm_grad = hidden_blocks(pre_grad, up_w)
            stream_grad = stream_grad + inv_rms * (norm_grad - normed * lax.optimization_barrier(jnp.mean(norm_grad * normed, axis=1, keepdims=True)))
    gradient = jnp.stack(grads)
    second = beta_two * path_rows[:, :, :, None] * path_cols[:, :, None, :] + (1.0 - beta_two) * gradient * gradient
    return (gradient / (jnp.sqrt(second) + adam_eps)).astype(jnp.bfloat16)

def reference(inputs, cotangent, path_table, slot_module, weights, momentum, row_factor, col_factor):
    module_range = jnp.arange(MODULES, dtype=jnp.int32)
    slot_of = lax.optimization_barrier(jnp.sum(jnp.where(slot_module[:, None] == module_range[None, :], module_range[:, None], 0), axis=0)).astype(jnp.int32)
    module_ids = (jnp.arange(LEVELS, dtype=jnp.int32)[None, :] * PER_LEVEL + path_table).astype(jnp.int32)
    slot_table = slot_of[module_ids].astype(jnp.int32)
    path_inputs = inputs.reshape(PATHS, TOK_PATH, D)
    path_cots = cotangent.reshape(PATHS, TOK_PATH, D)

    def one_path(running, packed):
        inputs_p, cot_p, slots_p, rows_p, cols_p = packed
        module_w = weights[slots_p]
        deltas = path_deltas(inputs_p, cot_p, module_w, rows_p, cols_p)
        for level in range(LEVELS):
            running = running.at[slots_p[level]].add(deltas[level].astype(jnp.float32))
        return (running, None)
    start = jnp.zeros((MODULES, 2, D, FF), jnp.float32)
    module_sums, unused = lax.scan(one_path, start, (path_inputs, path_cots, slot_table, row_factor, col_factor))
    counts = lax.optimization_barrier(jnp.sum((slot_table.reshape(-1)[None, :] == module_range[:, None]).astype(jnp.float32), axis=1))
    mean_delta = module_sums / jnp.maximum(counts, 1.0)[:, None, None, None]
    new_mom = momentum_mu * momentum.astype(jnp.float32) + mean_delta
    step_value = mean_delta + momentum_mu * new_mom
    return (new_mom.astype(jnp.bfloat16), step_value.astype(jnp.bfloat16))
```

```python
import functools

import jax
import jax.numpy as jnp
from jax import lax
from jax.experimental import pallas as pl
from jax.experimental.pallas import tpu as pltpu
from jax.sharding import PartitionSpec as P

norm_eps = 1e-06
beta_two = 0.95
adam_eps = 1e-08
momentum_mu = 0.9
MESH = pl.DeviceIdType.MESH


def gelu_tanh(values):
    return jax.nn.gelu(values, approximate=True)


def remote(src, dst, send, recv, device):
    return pltpu.make_async_remote_copy(
        src_ref=src,
        dst_ref=dst,
        send_sem=send,
        recv_sem=recv,
        device_id=device,
        device_id_type=MESH,
    )


def gather_kernel(n, chunks, w, o, own_sem, up_s, up_r, dn_s, dn_r, ys, yr, ps, pr, os, orr):
    p = lax.axis_index("paths")
    g = lax.axis_index("groups")
    k = lax.axis_index("pipe")
    above = {"paths": p + 1}
    below = {"paths": p - 1}
    twin = {"groups": 1 - g}
    core = {"pipe": 1 - k}
    size = w.shape[1] // chunks

    barrier = pltpu.get_barrier_semaphore()
    pl.semaphore_signal(barrier, inc=1, device_id=twin, device_id_type=MESH)
    pl.semaphore_signal(barrier, inc=1, device_id=core, device_id_type=MESH)

    @pl.when(p > 0)
    def _():
        pl.semaphore_signal(barrier, inc=1, device_id=below, device_id_type=MESH)

    @pl.when(p < n - 1)
    def _():
        pl.semaphore_signal(barrier, inc=1, device_id=above, device_id_type=MESH)

    pl.semaphore_wait(barrier, 2 + (p > 0).astype(jnp.int32) + (p < n - 1).astype(jnp.int32))

    def rows(c):
        return pl.ds(c * size, size)

    def spot(source, matrix, half, c):
        return o.at[source, matrix, half, rows(c)]

    def source(way, d):
        return p - d if way == 0 else p + d

    def present(way, d):
        return p - d >= 0 if way == 0 else p + d <= n - 1

    def onward(way, d):
        here = present(way, d)
        further = p < n - 1 if way == 0 else p > 0
        return further if d == 0 else jnp.logical_and(here, further)

    def chain(way, d, c):
        src = w.at[g, rows(c)] if d == 0 else spot(source(way, d), g, k, c)
        s, r = (up_s, up_r) if way == 0 else (dn_s, dn_r)
        return remote(
            src,
            spot(source(way, d), g, k, c),
            s.at[d, c],
            r.at[d, c],
            above if way == 0 else below,
        )

    def chain_in(way, d, c):
        s, r = (up_s, up_r) if way == 0 else (dn_s, dn_r)
        here = spot(source(way, d), g, k, c)
        return remote(here, here, s.at[d - 1, c], r.at[d - 1, c], below if way == 0 else above)

    def across(way, d, c):
        here = spot(source(way, d), g, k, c)
        return remote(here, here, ys.at[way, d - 1, c], yr.at[way, d - 1, c], twin)

    def across_in(way, d, c):
        here = spot(source(way, d), 1 - g, k, c)
        return remote(here, here, ys.at[way, d - 1, c], yr.at[way, d - 1, c], twin)

    def inner(kind, way, d, c):
        here = spot(source(way, d), g if kind == 0 else 1 - g, k, c)
        i = kind * 2 + way
        return remote(here, here, ps.at[i, d - 1, c], pr.at[i, d - 1, c], core)

    def inner_in(kind, way, d, c):
        here = spot(source(way, d), g if kind == 0 else 1 - g, 1 - k, c)
        i = kind * 2 + way
        return remote(here, here, ps.at[i, d - 1, c], pr.at[i, d - 1, c], core)

    for c in range(chunks):
        for way in range(2):

            @pl.when(onward(way, 0))
            def _():
                chain(way, 0, c).start()

    own = [pltpu.make_async_copy(w.at[j], o.at[p, j, k], own_sem.at[j]) for j in range(2)]
    own_out = [remote(w.at[j], o.at[p, j, k], os.at[j], orr.at[j], core) for j in range(2)]
    own_in = [
        remote(o.at[p, j, 1 - k], o.at[p, j, 1 - k], os.at[j], orr.at[j], core) for j in range(2)
    ]
    for j in range(2):
        own[j].start()
        own_out[j].start()

    steps = [(d, c) for d in range(1, n) for c in range(chunks)]
    lag = 2
    for i in range(len(steps) + lag):
        if i < len(steps):
            d, c = steps[i]
            for way in range(2):

                @pl.when(present(way, d))
                def _():
                    chain_in(way, d, c).wait_recv()
                    across(way, d, c).start()
                    inner(0, way, d, c).start()

                @pl.when(onward(way, d))
                def _():
                    chain(way, d, c).start()

        if i >= lag:
            d, c = steps[i - lag]
            for way in range(2):

                @pl.when(present(way, d))
                def _():
                    across_in(way, d, c).wait_recv()
                    inner(1, way, d, c).start()

    for j in range(2):
        own[j].wait()
        own_out[j].wait_send()
        own_in[j].wait_recv()
    for c in range(chunks):
        for way in range(2):
            for d in range(n):
                if d < n - 1:

                    @pl.when(onward(way, d))
                    def _():
                        chain(way, d, c).wait_send()

                if d > 0:

                    @pl.when(present(way, d))
                    def _():
                        across(way, d, c).wait_send()
                        for kind in range(2):
                            inner(kind, way, d, c).wait_send()
                            inner_in(kind, way, d, c).wait_recv()


def gather_modules(weights):
    n = lax.axis_size("paths")
    pipe = lax.axis_size("pipe")
    two, rows, hidden = weights.shape[1:]
    chunks = max(1, rows * hidden * 2 // (512 * 1024))
    dma = pltpu.SemaphoreType.DMA
    return pl.pallas_call(
        functools.partial(gather_kernel, n, chunks),
        out_shape=jax.ShapeDtypeStruct((n, two, pipe, rows, hidden), weights.dtype),
        in_specs=[pl.BlockSpec(memory_space=pl.ANY)],
        out_specs=pl.BlockSpec(memory_space=pl.ANY),
        scratch_shapes=[
            dma((2,)),
            dma((n - 1, chunks)),
            dma((n - 1, chunks)),
            dma((n - 1, chunks)),
            dma((n - 1, chunks)),
            dma((2, n - 1, chunks)),
            dma((2, n - 1, chunks)),
            dma((4, n - 1, chunks)),
            dma((4, n - 1, chunks)),
            dma((2,)),
            dma((2,)),
        ],
        compiler_params=pltpu.CompilerParams(collective_id=0, has_side_effects=True),
        cost_estimate=pl.CostEstimate(
            flops=0, bytes_accessed=n * two * pipe * rows * hidden * 16, transcendentals=0
        ),
        name="gather_modules",
    )(weights[0])


def reduce_kernel(n, levels, units, tile, w, d, out, up, dn, up_s, up_r, dn_s, dn_r):
    p = lax.axis_index("paths")
    above = {"paths": p + 1}
    below = {"paths": p - 1}
    chunks, rows = d.shape[1], d.shape[2]
    lag = 2

    barrier = pltpu.get_barrier_semaphore()

    @pl.when(p > 0)
    def _():
        pl.semaphore_signal(barrier, inc=1, device_id=below, device_id_type=MESH)

    @pl.when(p < n - 1)
    def _():
        pl.semaphore_signal(barrier, inc=1, device_id=above, device_id_type=MESH)

    pl.semaphore_wait(barrier, (p > 0).astype(jnp.int32) + (p < n - 1).astype(jnp.int32))

    def weight(who, level, j):
        return w[(who * levels + level) * (2 * n - 1) + j + n - 1]

    def parts(way):
        if way == 0:
            return up, up_s, up_r, above, below, 1, p, n - 1 - p
        return dn, dn_s, dn_r, below, above, 2, n - 1 - p, p

    def out_copy(way, u, c, src):
        land, s, r, to, _, _, _, _ = parts(way)
        return remote(src, land.at[u, c], s.at[u, c], r.at[u, c], to)

    def in_copy(way, u, c):
        land, s, r, _, frm, _, _, _ = parts(way)
        return remote(land.at[u, c], land.at[u, c], s.at[u, c], r.at[u, c], frm)

    def each_tile(body):
        def step(t, carry):
            body(pl.ds(pl.multiple_of(t * tile, tile), tile))
            return carry

        lax.fori_loop(0, rows // tile, step, 0)

    def own_part(c, t, j):
        total = d[0, c, t].astype(jnp.float32) * weight(0, 0, j)
        for level in range(1, levels):
            total += d[level, c, t].astype(jnp.float32) * weight(0, level, j)
        return total

    def flow(way, c):
        land, _, _, _, _, who, place, left = parts(way)
        sign = 1 if way == 0 else -1

        @pl.when(place == 1)
        def _():
            for u in range(levels):
                in_copy(way, u, c).wait_recv()

            def body(t):
                raw = [land[u, c, t].astype(jnp.float32) for u in range(levels)]

                def arrived(j):
                    total = raw[0] * weight(who, 0, sign * j)
                    for level in range(1, levels):
                        total += raw[level] * weight(who, level, sign * j)
                    return total

                out[c, t] += arrived(0)
                for j in range(1, n - 1):
                    land[j - 1, c, t] = (arrived(j) + own_part(c, t, sign * j)).astype(land.dtype)

            each_tile(body)
            for j in range(1, n - 1):
                out_copy(way, j - 1, c, land.at[j - 1, c]).start()

        @pl.when(place > 1)
        def _():
            for j in range(n - 2):

                @pl.when(j <= left)
                def _():
                    in_copy(way, j, c).wait_recv()

            def body(t):
                out[c, t] += land[0, c, t].astype(jnp.float32)

            each_tile(body)
            for j in range(1, n - 2):

                @pl.when(j <= left)
                def _():
                    def add(t):
                        land[j, c, t] = (
                            land[j, c, t].astype(jnp.float32) + own_part(c, t, sign * j)
                        ).astype(land.dtype)

                    each_tile(add)
                    out_copy(way, j - 1, c, land.at[j, c]).start()

    def raw_start(c, carry):
        @pl.when(p == 0)
        def _():
            for u in range(levels):
                out_copy(0, u, c, d.at[u, c]).start()

        @pl.when(p == n - 1)
        def _():
            for u in range(levels):
                out_copy(1, u, c, d.at[u, c]).start()

        return carry

    lax.fori_loop(0, chunks, raw_start, 0)

    low = p < n // 2
    late_up = jnp.where(low, 0, lag)
    late_dn = jnp.where(low, lag, 0)

    def step(i, carry):
        @pl.when(i < chunks)
        def _():
            def body(t):
                out[i, t] = own_part(i, t, 0)

            each_tile(body)

        c_up = i - late_up

        @pl.when(jnp.logical_and(c_up >= 0, c_up < chunks))
        def _():
            flow(0, c_up)

        c_dn = i - late_dn

        @pl.when(jnp.logical_and(c_dn >= 0, c_dn < chunks))
        def _():
            flow(1, c_dn)

        return carry

    lax.fori_loop(0, chunks + lag, step, 0)

    def drain(c, carry):
        for way in range(2):
            land, _, _, _, _, _, place, left = parts(way)

            @pl.when(place == 0)
            def _():
                for u in range(levels):
                    out_copy(way, u, c, d.at[u, c]).wait_send()

            @pl.when(place == 1)
            def _():
                for j in range(1, n - 1):
                    out_copy(way, j - 1, c, land.at[j - 1, c]).wait_send()

            @pl.when(place > 1)
            def _():
                for j in range(1, n - 2):

                    @pl.when(j <= left)
                    def _():
                        out_copy(way, j - 1, c, land.at[j, c]).wait_send()

        return carry

    lax.fori_loop(0, chunks, drain, 0)


def module_totals(shares, deltas):
    n = lax.axis_size("paths")
    levels, chunks, rows, hidden = deltas.shape
    units = max(levels, n - 2)
    dma = pltpu.SemaphoreType.DMA
    return pl.pallas_call(
        functools.partial(reduce_kernel, n, levels, units, 16),
        out_shape=jax.ShapeDtypeStruct((chunks, rows, hidden), jnp.float32),
        in_specs=[
            pl.BlockSpec(memory_space=pltpu.SMEM),
            pl.BlockSpec(memory_space=pltpu.VMEM),
        ],
        out_specs=pl.BlockSpec(memory_space=pltpu.VMEM),
        scratch_shapes=[
            pltpu.VMEM((units, chunks, rows, hidden), deltas.dtype),
            pltpu.VMEM((units, chunks, rows, hidden), deltas.dtype),
            dma((units, chunks)),
            dma((units, chunks)),
            dma((units, chunks)),
            dma((units, chunks)),
        ],
        compiler_params=pltpu.CompilerParams(
            collective_id=1, has_side_effects=True, vmem_limit_bytes=48 * 1024 * 1024
        ),
        name="module_totals",
    )(shares, deltas)


def swap(value, axis):
    return lax.ppermute(value, axis, [(0, 1), (1, 0)])


def width_sum(partial_value):
    sent = partial_value.astype(jnp.bfloat16)
    if lax.axis_size("mp") == 2:
        return sent.astype(jnp.float32) + swap(sent, "mp").astype(jnp.float32)
    return lax.psum(sent, "mp").astype(jnp.float32)


def local(inputs, cotangent, path_table, slot_module, weights, momentum, row_factor, col_factor):
    full_w = gather_modules(weights)
    stream_in, cot_full = (
        lax.all_gather(inputs, "mp", axis=1, tiled=True),
        lax.all_gather(cotangent, "mp", axis=1, tiled=True),
    )
    levels = path_table.shape[1]
    npaths = lax.axis_size("paths")
    p = lax.axis_index("paths")
    k = lax.axis_index("pipe")
    modules = slot_module.shape[0]
    per_level = modules // levels
    tokens, width = stream_in.shape
    half_rows = weights.shape[2]
    hidden = weights.shape[3]
    full_w = full_w.reshape(npaths, 2, width, hidden)
    module_range = jnp.arange(modules, dtype=jnp.int32)
    slot_of = jnp.sum(
        jnp.where(slot_module[:, None] == module_range[None, :], module_range[:, None], 0), axis=0
    )
    module_ids = jnp.arange(levels, dtype=jnp.int32)[None, :] * per_level + path_table
    slot_table = jnp.sum(
        jnp.where(module_ids[:, :, None] == module_range[None, None, :], slot_of[None, None, :], 0),
        axis=2,
    )
    own_slots = lax.dynamic_index_in_dim(slot_table, p, 0, keepdims=False)

    def matrix(level, j):
        return lax.dynamic_slice(
            full_w, (own_slots[level], j, 0, 0), (1, 1, width, hidden)
        ).reshape(width, hidden)

    def both_tokens(value):
        return jnp.concatenate([value, swap(value, "pipe")], axis=0)

    def own_rows(value):
        mine = lax.dynamic_slice(value, (0, k * half_rows), (tokens, half_rows))
        other = lax.dynamic_slice(value, (0, (1 - k) * half_rows), (tokens, half_rows))
        return jnp.concatenate([mine, swap(other, "pipe")], axis=0)

    def dot(left, right, dims):
        return lax.dot_general(left, right, (dims, ((), ())), preferred_element_type=jnp.float32)

    stream = stream_in.astype(jnp.float32)
    saved = []
    for level in range(levels):
        up_w, down_w = matrix(level, 0), matrix(level, 1)
        inv_rms = lax.rsqrt(jnp.mean(stream * stream, axis=1, keepdims=True) + norm_eps)
        normed = stream * inv_rms
        normed_b = normed.astype(jnp.bfloat16)
        pre_act = dot(normed_b, up_w, ((1,), (0,)))
        activated = gelu_tanh(pre_act).astype(jnp.bfloat16)
        saved.append((inv_rms, normed, normed_b, pre_act, activated, up_w, down_w))
        if level < levels - 1:
            stream = stream + width_sum(dot(activated, down_w, ((1,), (1,))))
    stream_grad = cot_full.astype(jnp.float32)
    deltas = [None] * levels

    def delta(gradient, level, j):
        second = (
            beta_two * row_factor[0, level, j][:, None] * col_factor[0, level, j][None, :]
            + (1.0 - beta_two) * gradient * gradient
        )
        return (gradient / (jnp.sqrt(second) + adam_eps)).astype(jnp.bfloat16)

    for level in reversed(range(levels)):
        inv_rms, normed, normed_b, pre_act, activated, up_w, down_w = saved[level]
        out_grad = stream_grad.astype(jnp.bfloat16)
        act_grad = dot(out_grad, down_w, ((1,), (0,)))
        pre_grad = jax.vjp(gelu_tanh, pre_act)[1](act_grad)[0].astype(jnp.bfloat16)
        if level > 0:
            norm_grad = width_sum(dot(pre_grad, up_w, ((1,), (1,))))
            stream_grad = stream_grad + inv_rms * (
                norm_grad - normed * jnp.mean(norm_grad * normed, axis=1, keepdims=True)
            )
        up_grad = dot(own_rows(normed_b), both_tokens(pre_grad), ((0,), (0,)))
        down_grad = dot(own_rows(out_grad), both_tokens(activated), ((0,), (0,)))
        deltas[level] = jnp.stack([delta(up_grad, level, 0), delta(down_grad, level, 1)])

    chunks = 16
    stacked = jnp.stack(deltas).reshape(levels, chunks, 2 * half_rows // chunks, hidden)
    offsets = p + jnp.arange(-(npaths - 1), npaths, dtype=jnp.int32)
    shares = jnp.stack(
        [
            (slots[:, None] == offsets[None, :]).astype(jnp.float32)
            for slots in (own_slots, slot_table[0], slot_table[npaths - 1])
        ]
    ).reshape(-1)
    totals = module_totals(shares, stacked).reshape(1, 2, half_rows, hidden)
    count = jnp.sum((slot_table == p).astype(jnp.float32))
    owned = totals / jnp.maximum(count, 1.0)
    new_mom = momentum_mu * momentum.astype(jnp.float32) + owned
    step_value = owned + momentum_mu * new_mom
    return (new_mom.astype(jnp.bfloat16), step_value.astype(jnp.bfloat16))


def solution(mesh):
    in_specs = (
        P(("groups", "paths", "pipe"), "mp"),
        P(("groups", "paths", "pipe"), "mp"),
        P("groups", None),
        P(),
        P("paths", None, "pipe", "mp"),
        P("paths", None, "pipe", "mp"),
        P(("groups", "paths"), None, None, "pipe"),
        P(("groups", "paths"), None, None, "mp"),
    )
    out_specs = (
        P(("groups", "paths"), None, "pipe", "mp"),
        P(("groups", "paths"), None, "pipe", "mp"),
    )
    return jax.shard_map(local, mesh=mesh, in_specs=in_specs, out_specs=out_specs, check_vma=False)
```

```python
import functools

import jax
import jax.numpy as jnp
from jax import lax
from jax.experimental import pallas as pl
from jax.experimental.pallas import tpu as pltpu
from jax.sharding import PartitionSpec as P

norm_eps = 1e-06
beta_two = 0.95
adam_eps = 1e-08
momentum_mu = 0.9
MESH = pl.DeviceIdType.MESH


def gelu_tanh(values):
    return jax.nn.gelu(values, approximate=True)


def remote(src, dst, send, recv, device):
    return pltpu.make_async_remote_copy(
        src_ref=src,
        dst_ref=dst,
        send_sem=send,
        recv_sem=recv,
        device_id=device,
        device_id_type=MESH,
    )


def greet(n, m_size, p, m, core):
    barrier = pltpu.get_barrier_semaphore()
    peers = [{"paths": lax.rem(p + e, n)} for e in range(1, n)]
    peers += [{"mp": lax.rem(m + f, m_size)} for f in range(1, m_size)]
    if core is not None:
        peers.append(core)
    for peer in peers:
        pl.semaphore_signal(barrier, inc=1, device_id=peer, device_id_type=MESH)
    pl.semaphore_wait(barrier, len(peers))


def spread_kernel(n, m_size, arrays, extras, *refs):
    ins, refs = refs[: arrays + extras], refs[arrays + extras :]
    outs, sems = refs[: arrays + extras], refs[arrays + extras :]
    own_s, zs, zr, xs, xr, ps, pr, es, er = sems
    p, m, k = lax.axis_index("paths"), lax.axis_index("mp"), lax.axis_index("pipe")
    core = {"pipe": 1 - k}
    greet(n, m_size, p, m, core)
    width = ins[0].shape[1]

    def spot(a, q, half, column):
        start = pl.multiple_of(column * width, 128)
        return outs[a].at[q, half, :, pl.ds(start, width)]

    def there(e):
        return lax.rem(p + e, n)

    def origin(e):
        return lax.rem(p + n - e, n)

    def column(f):
        return lax.rem(m + m_size - f, m_size)

    started, landed = [], []

    def begin(copy):
        copy.start()
        started.append(copy)

    local = []
    for a in range(arrays):
        for e in range(1, n):
            begin(
                remote(
                    ins[a],
                    spot(a, p, k, m),
                    zs.at[a, e - 1],
                    zr.at[a, e - 1],
                    {"paths": there(e)},
                )
            )

    def onward(a, e, src):
        q = origin(e) if e else p
        for f in range(1, m_size):
            begin(
                remote(
                    src,
                    spot(a, q, k, m),
                    xs.at[a, e, f - 1],
                    xr.at[a, e, f - 1],
                    {"mp": lax.rem(m + f, m_size)},
                )
            )
        begin(remote(src, spot(a, q, k, m), ps.at[a, e, 0], pr.at[a, e, 0], core))

    for a in range(arrays):
        onward(a, 0, ins[a])
        local.append(pltpu.make_async_copy(ins[a], spot(a, p, k, m), own_s.at[a]))
    if extras:
        row, col, w = ins[arrays:]
        row_o, col_o, w_o = outs[arrays:]
        local.append(pltpu.make_async_copy(row, row_o.at[p, k], own_s.at[arrays]))
        local.append(pltpu.make_async_copy(col, col_o.at[p], own_s.at[arrays + 1]))
        for e in range(1, n):
            to, q = {"paths": there(e)}, origin(e)
            begin(remote(row, row_o.at[p, k], es.at[0, e], er.at[0, e], to))
            begin(remote(col, col_o.at[p], es.at[1, e], er.at[1, e], to))
            landed.append(remote(col_o.at[q], col_o.at[q], es.at[1, e], er.at[1, e], to))
        begin(remote(row, row_o.at[p, k], es.at[2, 0], er.at[2, 0], core))
        for j in range(2):
            local.append(pltpu.make_async_copy(w.at[j], w_o.at[j, k], own_s.at[arrays + 2 + j]))
            begin(remote(w.at[j], w_o.at[j, k], es.at[3, j], er.at[3, j], core))
            here = w_o.at[j, 1 - k]
            landed.append(remote(here, here, es.at[3, j], er.at[3, j], core))
        for e in range(n):
            here = row_o.at[origin(e) if e else p, 1 - k]
            landed.append(remote(here, here, es.at[2, e], er.at[2, e], core))
    for copy in local:
        copy.start()

    for a in range(arrays):
        for e in range(1, n):
            here = spot(a, origin(e), k, m)
            remote(here, here, zs.at[a, e - 1], zr.at[a, e - 1], core).wait_recv()
            onward(a, e, here)
    if extras:
        for e in range(1, n):
            here = row_o.at[origin(e), k]
            remote(here, here, es.at[0, e], er.at[0, e], core).wait_recv()
            begin(remote(here, here, es.at[2, e], er.at[2, e], core))
    for a in range(arrays):
        for e in range(n):
            q = origin(e) if e else p
            for f in range(1, m_size):
                here = spot(a, q, k, column(f))
                remote(here, here, xs.at[a, e, f - 1], xr.at[a, e, f - 1], core).wait_recv()
                begin(remote(here, here, ps.at[a, e, f], pr.at[a, e, f], core))
            for f in range(m_size):
                here = spot(a, q, 1 - k, column(f))
                landed.append(remote(here, here, ps.at[a, e, f], pr.at[a, e, f], core))
    for copy in landed:
        copy.wait_recv()
    for copy in started:
        copy.wait_send()
    for copy in local:
        copy.wait()


def spread(values, extras, number):
    n, m_size, pipe = lax.axis_size("paths"), lax.axis_size("mp"), lax.axis_size("pipe")
    arrays = len(values)
    tokens, width = values[0].shape
    out = [
        jax.ShapeDtypeStruct((n, pipe, tokens, width * m_size), value.dtype) for value in values
    ]
    if extras:
        row, col, w = extras
        out.append(jax.ShapeDtypeStruct((n, pipe) + row.shape, row.dtype))
        out.append(jax.ShapeDtypeStruct((n,) + col.shape, col.dtype))
        out.append(jax.ShapeDtypeStruct((2, pipe) + w.shape[1:], w.dtype))
    dma = pltpu.SemaphoreType.DMA
    anywhere = pl.BlockSpec(memory_space=pl.ANY)
    return pl.pallas_call(
        functools.partial(spread_kernel, n, m_size, arrays, len(extras)),
        out_shape=out,
        in_specs=[anywhere] * (arrays + len(extras)),
        out_specs=[anywhere] * (arrays + len(extras)),
        scratch_shapes=[
            dma((arrays + 4,)),
            dma((arrays, n - 1)),
            dma((arrays, n - 1)),
            dma((arrays, n, m_size - 1)),
            dma((arrays, n, m_size - 1)),
            dma((arrays, n, m_size)),
            dma((arrays, n, m_size)),
            dma((4, n)),
            dma((4, n)),
        ],
        compiler_params=pltpu.CompilerParams(collective_id=number, has_side_effects=True),
        name="spread_" + str(number),
    )(*values, *extras)


def collect_kernel(n, m_size, tile, y, out, xl, zs, zl, xs, xr, ss, sr):
    p, m = lax.axis_index("paths"), lax.axis_index("mp")
    greet(n, m_size, p, m, None)
    tokens, width = out.shape

    def columns(block):
        return pl.ds(pl.multiple_of(block * width, 128), width)

    def path(e):
        return lax.rem(p + e, n)

    order = list(range(1, n)) + [0]
    started = []
    for e in order:
        for f in range(1, m_size):
            to = lax.rem(m + f, m_size)
            copy = remote(
                y.at[path(e), :, columns(to)],
                xl.at[e, f - 1],
                xs.at[e, f - 1],
                xr.at[e, f - 1],
                {"mp": to},
            )
            copy.start()
            started.append(copy)

    def each_tile(body):
        def step(t, carry):
            body(pl.ds(pl.multiple_of(t * tile, tile), tile))
            return carry

        lax.fori_loop(0, tokens // tile, step, 0)

    def summed(e, t):
        total = y[path(e), t, columns(m)].astype(jnp.float32)
        for f in range(1, m_size):
            total += xl[e, f - 1, t].astype(jnp.float32)
        return total

    for e in order:
        for f in range(1, m_size):
            here = xl.at[e, f - 1]
            remote(here, here, xs.at[e, f - 1], xr.at[e, f - 1], {"mp": m}).wait_recv()
        if e:

            def body(t):
                zs[e - 1, t] = summed(e, t).astype(zs.dtype)

            each_tile(body)
            copy = remote(
                zs.at[e - 1], zl.at[e - 1], ss.at[e - 1], sr.at[e - 1], {"paths": path(e)}
            )
            copy.start()
            started.append(copy)
    for e in range(1, n):
        here = zl.at[e - 1]
        remote(here, here, ss.at[e - 1], sr.at[e - 1], {"paths": p}).wait_recv()

    def finish(t):
        total = summed(0, t)
        for e in range(1, n):
            total += zl[e - 1, t].astype(jnp.float32)
        out[t] = total

    each_tile(finish)
    for copy in started:
        copy.wait_send()


def collect(y, number):
    n, m_size = lax.axis_size("paths"), lax.axis_size("mp")
    _, tokens, features = y.shape
    width = features // m_size
    dma = pltpu.SemaphoreType.DMA
    return pl.pallas_call(
        functools.partial(collect_kernel, n, m_size, 32),
        out_shape=jax.ShapeDtypeStruct((tokens, width), jnp.float32),
        in_specs=[pl.BlockSpec(memory_space=pltpu.VMEM)],
        out_specs=pl.BlockSpec(memory_space=pltpu.VMEM),
        scratch_shapes=[
            pltpu.VMEM((n, m_size - 1, tokens, width), y.dtype),
            pltpu.VMEM((n - 1, tokens, width), y.dtype),
            pltpu.VMEM((n - 1, tokens, width), y.dtype),
            dma((n, m_size - 1)),
            dma((n, m_size - 1)),
            dma((n - 1,)),
            dma((n - 1,)),
        ],
        compiler_params=pltpu.CompilerParams(
            collective_id=number, has_side_effects=True, vmem_limit_bytes=40 * 1024 * 1024
        ),
        name="collect_" + str(number),
    )(y)


def swap(value, axis):
    return lax.ppermute(value, axis, [(0, 1), (1, 0)])


def feature_sum(value):
    partial_sum = jnp.sum(value, axis=1, keepdims=True)
    if lax.axis_size("mp") == 2:
        return partial_sum + swap(partial_sum, "mp")
    return lax.psum(partial_sum, "mp")


def dot(left, right, dims):
    return lax.dot_general(left, right, (dims, ((), ())), preferred_element_type=jnp.float32)


def local(inputs, cotangent, path_table, slot_module, weights, momentum, row_factor, col_factor):
    levels = path_table.shape[1]
    n = lax.axis_size("paths")
    pipe = lax.axis_size("pipe")
    p = lax.axis_index("paths")
    k = lax.axis_index("pipe")
    modules = slot_module.shape[0]
    per_level = modules // levels
    tokens, block = inputs.shape
    half_rows, hidden = weights.shape[2:]
    width = half_rows * pipe
    quarter = hidden // pipe
    module_range = jnp.arange(modules, dtype=jnp.int32)
    own_module = jnp.sum(jnp.where(module_range == p, slot_module, 0))
    own_level = own_module // per_level
    module_ids = jnp.arange(levels, dtype=jnp.int32)[None, :] * per_level + path_table
    chosen = (module_ids == own_module).astype(jnp.float32)

    inputs_all, cot_all, rows_all, cols_all, full_w = spread(
        (inputs, cotangent),
        (row_factor.reshape(-1, 128), col_factor.reshape(-1, 128), weights[0]),
        0,
    )
    up_w = full_w[0].reshape(width, hidden)
    down_w = full_w[1].reshape(width, hidden)

    def own_tokens(value):
        return lax.dynamic_index_in_dim(value, k, 1, keepdims=False).reshape(n * tokens, width)

    def offered(value, level):
        value = value.reshape(n, tokens, width) * chosen[:, level][:, None, None]
        return value.astype(jnp.bfloat16)

    stream_all = inputs_all.astype(jnp.float32)
    normed_all = (
        stream_all
        * lax.rsqrt(jnp.mean(stream_all * stream_all, axis=3, keepdims=True) + norm_eps)
    ).astype(jnp.bfloat16)
    activated = gelu_tanh(dot(own_tokens(normed_all), up_w, ((1,), (0,)))).astype(jnp.bfloat16)
    output = collect(offered(dot(activated, down_w, ((1,), (1,))), 0), 1)

    stream = inputs.astype(jnp.float32) + output
    inv_rms = lax.rsqrt(feature_sum(stream * stream) / width + norm_eps)
    normed = stream * inv_rms
    (last_all,) = spread((normed.astype(jnp.bfloat16),), (), 2)
    act_grad = dot(own_tokens(cot_all), down_w, ((1,), (0,)))
    pre_act = dot(own_tokens(last_all), up_w, ((1,), (0,)))
    pre_grad = jax.vjp(gelu_tanh, pre_act)[1](act_grad)[0].astype(jnp.bfloat16)
    norm_grad = collect(offered(dot(pre_grad, up_w, ((1,), (1,))), 1), 3)
    stream_grad = cotangent.astype(jnp.float32) + inv_rms * (
        norm_grad - normed * (feature_sum(norm_grad * normed) / width)
    )
    (first_all,) = spread((stream_grad.astype(jnp.bfloat16),), (), 4)

    at_first = own_level == 0
    left = jnp.where(at_first, normed_all, last_all).reshape(n * pipe * tokens, width)
    right = jnp.where(at_first, first_all, cot_all).reshape(n * pipe * tokens, width)
    up_q = lax.dynamic_slice(up_w, (0, k * quarter), (width, quarter))
    down_q = lax.dynamic_slice(down_w, (0, k * quarter), (width, quarter))
    pre_act = dot(left, up_q, ((1,), (0,)))
    activated = gelu_tanh(pre_act).astype(jnp.bfloat16)
    act_grad = dot(right, down_q, ((1,), (0,)))
    pre_grad = jax.vjp(gelu_tanh, pre_act)[1](act_grad)[0].astype(jnp.bfloat16)

    rows = lax.dynamic_index_in_dim(
        rows_all.reshape(n, pipe, levels, 2, half_rows), own_level, 2, keepdims=False
    )
    rows = jnp.transpose(rows, (0, 2, 1, 3)).reshape(n, 2, width)
    cols = lax.dynamic_slice(
        cols_all.reshape(n, levels, 2, hidden), (0, own_level, 0, k * quarter), (n, 1, 2, quarter)
    ).reshape(n, 2, quarter)
    shares = lax.dynamic_index_in_dim(chosen, own_level, 1, keepdims=False)
    count = jnp.maximum(jnp.sum(chosen), 1.0)
    path_tokens = pipe * tokens
    means = []
    for j, (a, b) in enumerate(((left, pre_grad), (right, activated))):
        total = 0.0
        for q in range(n):
            span = slice(q * path_tokens, (q + 1) * path_tokens)
            gradient = dot(a[span], b[span], ((0,), (0,)))
            second = (
                beta_two * rows[q, j][:, None] * cols[q, j][None, :]
                + (1.0 - beta_two) * gradient * gradient
            )
            delta = (gradient / (jnp.sqrt(second) + adam_eps)).astype(jnp.bfloat16)
            total = total + delta.astype(jnp.float32) * shares[q]
        means.append((total / count).astype(jnp.bfloat16))
    mean = jnp.stack(means)
    mine = lax.dynamic_slice(mean, (0, k * half_rows, 0), (2, half_rows, quarter))
    sent = lax.dynamic_slice(mean, (0, (1 - k) * half_rows, 0), (2, half_rows, quarter))
    other = swap(sent, "pipe")
    owned = jnp.where(
        k == 0,
        jnp.concatenate([mine, other], axis=2),
        jnp.concatenate([other, mine], axis=2),
    ).astype(jnp.float32)
    new_mom = momentum_mu * momentum.astype(jnp.float32) + owned[None]
    step_value = owned[None] + momentum_mu * new_mom
    return (new_mom.astype(jnp.bfloat16), step_value.astype(jnp.bfloat16))


def solution(mesh):
    in_specs = (
        P(("groups", "paths", "pipe"), "mp"),
        P(("groups", "paths", "pipe"), "mp"),
        P("groups", None),
        P(),
        P("paths", None, "pipe", "mp"),
        P("paths", None, "pipe", "mp"),
        P(("groups", "paths"), None, None, "pipe"),
        P(("groups", "paths"), None, None, "mp"),
    )
    out_specs = (
        P(("groups", "paths"), None, "pipe", "mp"),
        P(("groups", "paths"), None, "pipe", "mp"),
    )
    return jax.shard_map(local, mesh=mesh, in_specs=in_specs, out_specs=out_specs, check_vma=False)
```

```python
import functools

import jax
import jax.numpy as jnp
from jax import lax
from jax.experimental import pallas as pl
from jax.experimental.layout import Layout, with_layout_constraint
from jax.experimental.pallas import tpu as pltpu
from jax.sharding import PartitionSpec as P

norm_eps = 1e-06
beta_two = 0.95
adam_eps = 1e-08
momentum_mu = 0.9
MESH = pl.DeviceIdType.MESH


def gelu_tanh(values):
    return jax.nn.gelu(values, approximate=True)


def remote(src, dst, send, recv, device):
    return pltpu.make_async_remote_copy(
        src_ref=src,
        dst_ref=dst,
        send_sem=send,
        recv_sem=recv,
        device_id=device,
        device_id_type=MESH,
    )


def greet(n, m_size, p, m, core):
    barrier = pltpu.get_barrier_semaphore()
    peers = [{"paths": lax.rem(p + e, n)} for e in range(1, n)]
    peers += [{"mp": lax.rem(m + f, m_size)} for f in range(1, m_size)]
    if core is not None:
        peers.append(core)
    for peer in peers:
        pl.semaphore_signal(barrier, inc=1, device_id=peer, device_id_type=MESH)
    pl.semaphore_wait(barrier, len(peers))


def spread_kernel(n, m_size, arrays, extras, *refs):
    ins, refs = refs[: arrays + extras], refs[arrays + extras :]
    outs, sems = refs[: arrays + extras], refs[arrays + extras :]
    own_s, zs, zr, xs, xr, ps, pr, es, er = sems
    p, m, k = lax.axis_index("paths"), lax.axis_index("mp"), lax.axis_index("pipe")
    core = {"pipe": 1 - k}
    greet(n, m_size, p, m, core)
    width = ins[0].shape[1]

    def spot(a, q, half, column):
        start = pl.multiple_of(column * width, 128)
        return outs[a].at[q, half, :, pl.ds(start, width)]

    def there(e):
        return lax.rem(p + e, n)

    def origin(e):
        return lax.rem(p + n - e, n)

    def column(f):
        return lax.rem(m + m_size - f, m_size)

    started, landed = [], []

    def begin(copy):
        copy.start()
        started.append(copy)

    local = []
    for a in range(arrays):
        for e in range(1, n):
            begin(
                remote(
                    ins[a],
                    spot(a, p, k, m),
                    zs.at[a, e - 1],
                    zr.at[a, e - 1],
                    {"paths": there(e)},
                )
            )

    def onward(a, e, src):
        q = origin(e) if e else p
        for f in range(1, m_size):
            begin(
                remote(
                    src,
                    spot(a, q, k, m),
                    xs.at[a, e, f - 1],
                    xr.at[a, e, f - 1],
                    {"mp": lax.rem(m + f, m_size)},
                )
            )
        begin(remote(src, spot(a, q, k, m), ps.at[a, e, 0], pr.at[a, e, 0], core))

    for a in range(arrays):
        onward(a, 0, ins[a])
        local.append(pltpu.make_async_copy(ins[a], spot(a, p, k, m), own_s.at[a]))
    if extras:
        row, col = ins[arrays:]
        row_o, col_o = outs[arrays:]
        local.append(pltpu.make_async_copy(row, row_o.at[p, k], own_s.at[arrays]))
        local.append(pltpu.make_async_copy(col, col_o.at[p], own_s.at[arrays + 1]))
        for e in range(1, n):
            to, q = {"paths": there(e)}, origin(e)
            begin(remote(row, row_o.at[p, k], es.at[0, e], er.at[0, e], to))
            begin(remote(col, col_o.at[p], es.at[1, e], er.at[1, e], to))
            landed.append(remote(col_o.at[q], col_o.at[q], es.at[1, e], er.at[1, e], to))
        begin(remote(row, row_o.at[p, k], es.at[2, 0], er.at[2, 0], core))
        for e in range(n):
            here = row_o.at[origin(e) if e else p, 1 - k]
            landed.append(remote(here, here, es.at[2, e], er.at[2, e], core))
    for copy in local:
        copy.start()

    for a in range(arrays):
        for e in range(1, n):
            here = spot(a, origin(e), k, m)
            remote(here, here, zs.at[a, e - 1], zr.at[a, e - 1], core).wait_recv()
            onward(a, e, here)
    if extras:
        for e in range(1, n):
            here = row_o.at[origin(e), k]
            remote(here, here, es.at[0, e], er.at[0, e], core).wait_recv()
            begin(remote(here, here, es.at[2, e], er.at[2, e], core))
    for a in range(arrays):
        for e in range(n):
            q = origin(e) if e else p
            for f in range(1, m_size):
                here = spot(a, q, k, column(f))
                remote(here, here, xs.at[a, e, f - 1], xr.at[a, e, f - 1], core).wait_recv()
                begin(remote(here, here, ps.at[a, e, f], pr.at[a, e, f], core))
            for f in range(m_size):
                here = spot(a, q, 1 - k, column(f))
                landed.append(remote(here, here, ps.at[a, e, f], pr.at[a, e, f], core))
    for copy in landed:
        copy.wait_recv()
    for copy in started:
        copy.wait_send()
    for copy in local:
        copy.wait()


def spread(values, extras, number):
    n, m_size, pipe = lax.axis_size("paths"), lax.axis_size("mp"), lax.axis_size("pipe")
    arrays = len(values)
    tokens, width = values[0].shape
    out = [
        jax.ShapeDtypeStruct((n, pipe, tokens, width * m_size), value.dtype) for value in values
    ]
    if extras:
        row, col = extras
        out.append(jax.ShapeDtypeStruct((n, pipe) + row.shape, row.dtype))
        out.append(jax.ShapeDtypeStruct((n,) + col.shape, col.dtype))
    dma = pltpu.SemaphoreType.DMA
    anywhere = pl.BlockSpec(memory_space=pl.ANY)
    return pl.pallas_call(
        functools.partial(spread_kernel, n, m_size, arrays, len(extras)),
        out_shape=out,
        in_specs=[anywhere] * (arrays + len(extras)),
        out_specs=[anywhere] * (arrays + len(extras)),
        scratch_shapes=[
            dma((arrays + 2,)),
            dma((arrays, n - 1)),
            dma((arrays, n - 1)),
            dma((arrays, n, m_size - 1)),
            dma((arrays, n, m_size - 1)),
            dma((arrays, n, m_size)),
            dma((arrays, n, m_size)),
            dma((3, n)),
            dma((3, n)),
        ],
        compiler_params=pltpu.CompilerParams(collective_id=number, has_side_effects=True),
        name="spread_" + str(number),
    )(*values, *extras)


def collect_kernel(n, m_size, tile, y, out, xl, zs, zl, xs, xr, ss, sr):
    p, m = lax.axis_index("paths"), lax.axis_index("mp")
    greet(n, m_size, p, m, None)
    tokens, width = out.shape

    def columns(block):
        return pl.ds(pl.multiple_of(block * width, 128), width)

    def path(e):
        return lax.rem(p + e, n)

    order = list(range(1, n)) + [0]
    started = []
    for e in order:
        for f in range(1, m_size):
            to = lax.rem(m + f, m_size)
            copy = remote(
                y.at[path(e), :, columns(to)],
                xl.at[e, f - 1],
                xs.at[e, f - 1],
                xr.at[e, f - 1],
                {"mp": to},
            )
            copy.start()
            started.append(copy)

    def each_tile(body):
        def step(t, carry):
            body(pl.ds(pl.multiple_of(t * tile, tile), tile))
            return carry

        lax.fori_loop(0, tokens // tile, step, 0)

    def summed(e, t):
        total = y[path(e), t, columns(m)].astype(jnp.float32)
        for f in range(1, m_size):
            total += xl[e, f - 1, t].astype(jnp.float32)
        return total

    for e in order:
        for f in range(1, m_size):
            here = xl.at[e, f - 1]
            remote(here, here, xs.at[e, f - 1], xr.at[e, f - 1], {"mp": m}).wait_recv()
        if e:

            def body(t):
                zs[e - 1, t] = summed(e, t).astype(zs.dtype)

            each_tile(body)
            copy = remote(
                zs.at[e - 1], zl.at[e - 1], ss.at[e - 1], sr.at[e - 1], {"paths": path(e)}
            )
            copy.start()
            started.append(copy)
    for e in range(1, n):
        here = zl.at[e - 1]
        remote(here, here, ss.at[e - 1], sr.at[e - 1], {"paths": p}).wait_recv()

    def finish(t):
        total = summed(0, t)
        for e in range(1, n):
            total += zl[e - 1, t].astype(jnp.float32)
        out[t] = total

    each_tile(finish)
    for copy in started:
        copy.wait_send()


def collect(y, number):
    n, m_size = lax.axis_size("paths"), lax.axis_size("mp")
    _, tokens, features = y.shape
    width = features // m_size
    dma = pltpu.SemaphoreType.DMA
    return pl.pallas_call(
        functools.partial(collect_kernel, n, m_size, 32),
        out_shape=jax.ShapeDtypeStruct((tokens, width), jnp.float32),
        in_specs=[pl.BlockSpec(memory_space=pltpu.VMEM)],
        out_specs=pl.BlockSpec(memory_space=pltpu.VMEM),
        scratch_shapes=[
            pltpu.VMEM((n, m_size - 1, tokens, width), y.dtype),
            pltpu.VMEM((n - 1, tokens, width), y.dtype),
            pltpu.VMEM((n - 1, tokens, width), y.dtype),
            dma((n, m_size - 1)),
            dma((n, m_size - 1)),
            dma((n - 1,)),
            dma((n - 1,)),
        ],
        compiler_params=pltpu.CompilerParams(
            collective_id=number, has_side_effects=True, vmem_limit_bytes=40 * 1024 * 1024
        ),
        name="collect_" + str(number),
    )(y)


def swap(value, axis):
    return lax.ppermute(value, axis, [(0, 1), (1, 0)])


def feature_sum(value):
    partial_sum = jnp.sum(value, axis=1, keepdims=True)
    if lax.axis_size("mp") == 2:
        return partial_sum + swap(partial_sum, "mp")
    return lax.psum(partial_sum, "mp")


def dot(left, right, dims):
    return lax.dot_general(left, right, (dims, ((), ())), preferred_element_type=jnp.float32)


def local(inputs, cotangent, path_table, slot_module, weights, momentum, row_factor, col_factor):
    levels = path_table.shape[1]
    n = lax.axis_size("paths")
    pipe = lax.axis_size("pipe")
    p = lax.axis_index("paths")
    k = lax.axis_index("pipe")
    modules = slot_module.shape[0]
    per_level = modules // levels
    tokens, block = inputs.shape
    half_rows, hidden = weights.shape[2:]
    width = half_rows * pipe
    quarter = hidden // pipe
    module_range = jnp.arange(modules, dtype=jnp.int32)
    own_module = jnp.sum(jnp.where(module_range == p, slot_module, 0))
    own_level = own_module // per_level
    module_ids = jnp.arange(levels, dtype=jnp.int32)[None, :] * per_level + path_table
    chosen = (module_ids == own_module).astype(jnp.float32)

    other_w = swap(weights[0], "pipe")
    inputs_all, cot_all, rows_all, cols_all = spread(
        (inputs, cotangent),
        (row_factor.reshape(-1, 128), col_factor.reshape(-1, 128)),
        0,
    )
    own_w = weights[0]
    up_w, down_w = (
        jnp.where(
            k == 0,
            jnp.concatenate([own_w[j], other_w[j]], axis=0),
            jnp.concatenate([other_w[j], own_w[j]], axis=0),
        )
        for j in range(2)
    )

    def own_tokens(value):
        return lax.dynamic_index_in_dim(value, k, 1, keepdims=False).reshape(n * tokens, width)

    def offered(value, level):
        value = value.reshape(n, tokens, width) * chosen[:, level][:, None, None]
        return value.astype(jnp.bfloat16)

    stream_all = inputs_all.astype(jnp.float32)
    normed_all = (
        stream_all
        * lax.rsqrt(jnp.mean(stream_all * stream_all, axis=3, keepdims=True) + norm_eps)
    ).astype(jnp.bfloat16)
    activated = gelu_tanh(dot(own_tokens(normed_all), up_w, ((1,), (0,)))).astype(jnp.bfloat16)
    output = collect(offered(dot(activated, down_w, ((1,), (1,))), 0), 1)

    stream = inputs.astype(jnp.float32) + output
    inv_rms = lax.rsqrt(feature_sum(stream * stream) / width + norm_eps)
    normed = stream * inv_rms
    (last_all,) = spread((normed.astype(jnp.bfloat16),), (), 2)
    act_grad = dot(own_tokens(cot_all), down_w, ((1,), (0,)))
    pre_act = dot(own_tokens(last_all), up_w, ((1,), (0,)))
    pre_grad = jax.vjp(gelu_tanh, pre_act)[1](act_grad)[0].astype(jnp.bfloat16)
    norm_grad = collect(offered(dot(pre_grad, up_w, ((1,), (1,))), 1), 3)
    stream_grad = cotangent.astype(jnp.float32) + inv_rms * (
        norm_grad - normed * (feature_sum(norm_grad * normed) / width)
    )
    (first_all,) = spread((stream_grad.astype(jnp.bfloat16),), (), 4)

    at_first = own_level == 0
    left = jnp.where(at_first, normed_all, last_all).reshape(n * pipe * tokens, width)
    right = jnp.where(at_first, first_all, cot_all).reshape(n * pipe * tokens, width)
    up_q = lax.dynamic_slice(up_w, (0, k * quarter), (width, quarter))
    down_q = lax.dynamic_slice(down_w, (0, k * quarter), (width, quarter))
    pre_act = dot(left, up_q, ((1,), (0,)))
    activated = gelu_tanh(pre_act).astype(jnp.bfloat16)
    act_grad = dot(right, down_q, ((1,), (0,)))
    pre_grad = jax.vjp(gelu_tanh, pre_act)[1](act_grad)[0].astype(jnp.bfloat16)

    rows = lax.dynamic_index_in_dim(
        rows_all.reshape(n, pipe, levels, 2, half_rows), own_level, 2, keepdims=False
    )
    rows = jnp.transpose(rows, (0, 2, 1, 3)).reshape(n, 2, width)
    cols = lax.dynamic_slice(
        cols_all.reshape(n, levels, 2, hidden), (0, own_level, 0, k * quarter), (n, 1, 2, quarter)
    ).reshape(n, 2, quarter)
    shares = lax.dynamic_index_in_dim(chosen, own_level, 1, keepdims=False)
    count = jnp.maximum(jnp.sum(chosen), 1.0)
    path_tokens = pipe * tokens
    means = []
    for j, (a, b) in enumerate(((left, pre_grad), (right, activated))):
        total = 0.0
        for q in range(n):
            span = slice(q * path_tokens, (q + 1) * path_tokens)
            gradient = dot(a[span], b[span], ((0,), (0,)))
            second = (
                beta_two * rows[q, j][:, None] * cols[q, j][None, :]
                + (1.0 - beta_two) * gradient * gradient
            )
            delta = (gradient / (jnp.sqrt(second) + adam_eps)).astype(jnp.bfloat16)
            total = total + delta.astype(jnp.float32) * shares[q]
        means.append((total / count).astype(jnp.bfloat16))
    mean = with_layout_constraint(jnp.stack(means), Layout(major_to_minor=(0, 1, 2)))
    mine = lax.dynamic_slice(mean, (0, k * half_rows, 0), (2, half_rows, quarter))
    sent = lax.dynamic_slice(mean, (0, (1 - k) * half_rows, 0), (2, half_rows, quarter))
    other = swap(sent, "pipe")
    owned = jnp.where(
        k == 0,
        jnp.concatenate([mine, other], axis=2),
        jnp.concatenate([other, mine], axis=2),
    ).astype(jnp.float32)
    new_mom = momentum_mu * momentum.astype(jnp.float32) + owned[None]
    step_value = owned[None] + momentum_mu * new_mom
    return (new_mom.astype(jnp.bfloat16), step_value.astype(jnp.bfloat16))


def solution(mesh):
    in_specs = (
        P(("groups", "paths", "pipe"), "mp"),
        P(("groups", "paths", "pipe"), "mp"),
        P("groups", None),
        P(),
        P("paths", None, "pipe", "mp"),
        P("paths", None, "pipe", "mp"),
        P(("groups", "paths"), None, None, "pipe"),
        P(("groups", "paths"), None, None, "mp"),
    )
    out_specs = (
        P(("groups", "paths"), None, "pipe", "mp"),
        P(("groups", "paths"), None, "pipe", "mp"),
    )
    return jax.shard_map(local, mesh=mesh, in_specs=in_specs, out_specs=out_specs, check_vma=False)
```
